256 devices in a mesh: grp: 16 (over y, x_lo, core), blk: 16 (over x_hi, z).
Axes of the slice: x: 4 (x_hi: 2, x_lo: 2; x = x_hi * 2 + x_lo), y: 4, z: 8, core: 2. Of those that a mesh axis runs over, the one named last changes fastest.
Arguments:
- patches: bfloat16 [2048, 64, 1152], P(('grp', 'blk')), may hold values from -200 to 200
- probe: bfloat16 [1152], replicated, may hold values from -4 to 4
- w_key: bfloat16 [1152, 1152], P('grp'), may hold values from -0.125 to 1.125
- w_value: bfloat16 [1152, 1152], P('grp'), may hold values from -0.1875 to 0.1875
- w_out: bfloat16 [1152, 1152], P('grp'), may hold values from -0.1875 to 0.1875
- texts: bfloat16 [2048, 1152], P(('grp', 'blk')), may hold values from -4 to 4
Outputs:
- grad_image: float32 [2048, 1152], P(('grp', 'blk'))
- grad_text: float32 [2048, 1152], P(('grp', 'blk'))
The draws below stay inside these ranges and needn't reach their ends.
All inputs are finite; a program needn't handle non-finite values.
Results may differ from the reference program's by a relative error of at most 0.0095.
Values may be sent and summed in bfloat16 or wider, within the bound.
A program may use at most 64 MiB of HBM per device.

```python
import math
import jax
import jax.numpy as jnp
from jax import lax

D = 1152
HEADS = 16
PATCH = 64
GROUP = 128
BATCH = 2048
N_GRP = 16


def probe_vector(key):
    return jnp.clip(jax.random.normal(jax.random.fold_in(key, 101), (D,), jnp.float32), -4.0, 4.0)


def log_spread(key, count, lower, upper):
    return jnp.exp(jax.random.uniform(key, (count,), jnp.float32, jnp.log(lower), jnp.log(upper)))


def draw_probe(key, part):
    shared = probe_vector(key)
    return shared.astype(jnp.bfloat16)


def draw_patches(key, part):
    key = jax.random.fold_in(key, 2)
    streams = jax.random.split(key, 3)
    column = log_spread(streams[0], D, 0.3, 3.0)
    image_scale = log_spread(streams[1], BATCH, 0.05, 0.5)
    base = jnp.clip(jax.random.normal(streams[2], (BATCH, PATCH, D), jnp.float32), -4.0, 4.0)
    field = base * image_scale[:, None, None] * column[None, None, :]
    return field.astype(jnp.bfloat16)


def draw_w_key(key, part):
    key = jax.random.fold_in(key, 3)
    noise = jax.random.normal(key, (D, D), jnp.float32) / jnp.sqrt(jnp.float32(D))
    noise = jnp.clip(noise, -0.125, 0.125)
    return (jnp.eye(D, dtype=jnp.float32) + noise).astype(jnp.bfloat16)


def draw_texts(key, part):
    key = jax.random.fold_in(key, 4)
    streams = jax.random.split(key, 3)
    column = log_spread(streams[0], D, 0.3, 3.0)
    row_scale = log_spread(streams[1], BATCH, 0.02, 0.2)
    base = jnp.clip(jax.random.normal(streams[2], (BATCH, D), jnp.float32), -4.0, 4.0)
    return (base * row_scale[:, None] * column[None, :]).astype(jnp.bfloat16)


def level_of(key, shape, shards, smallest, top_value):
    def one(position, blocks):
        steps = jax.random.uniform(jax.random.fold_in(jax.random.fold_in(key, 6), position), (blocks,), jnp.float32, smallest / len(shards), top_value / len(shards))
        return jnp.repeat(jnp.exp(steps), shape[position] // blocks).reshape((-1,) + (1,) * (len(shape) - position - 1))

    level = one(*shards[0])
    for cut in shards[1:]:
        level = level * one(*cut)
    return level


def normal_values(key, dims, scale, most, shards=(), kind=jnp.bfloat16):
    array = scale * jax.random.normal(key, dims, jnp.float32)
    if shards:
        array = array * level_of(key, dims, shards, -0.22, 0.18)
    return jnp.clip(array, -most, most).astype(kind)


def setup_inputs(seed: int = 0) -> dict:
    seeds = jax.random.split(jax.random.key(seed), 7)
    return {
        "patches": draw_patches(jax.random.fold_in(seeds[6], 71), 0),
        "probe": draw_probe(jax.random.fold_in(seeds[6], 71), 0),
        "w_key": draw_w_key(jax.random.fold_in(seeds[6], 71), 0),
        "w_value": normal_values(seeds[3], (D, D), D ** -0.5, 0.1875, ((0, 16),)),
        "w_out": normal_values(seeds[4], (D, D), D ** -0.5, 0.1875, ((0, 16),)),
        "texts": draw_texts(jax.random.fold_in(seeds[6], 71), 0),
    }


def head_table():
    head_size = D // HEADS
    owner = jnp.arange(D, dtype=jnp.int32) // head_size
    return (owner[:, None] == jnp.arange(HEADS, dtype=jnp.int32)[None, :]).astype(jnp.float32)

def unit_rows(values):
    inverse = lax.rsqrt(lax.optimization_barrier(jnp.sum(values * values, axis=1, keepdims=True)) + 1e-06)
    return (values * inverse, inverse)

def chain_back(grad_unit, unit_f, inverse):
    inner = lax.optimization_barrier(jnp.sum(unit_f * grad_unit, axis=1, keepdims=True))
    return (grad_unit - unit_f * inner) * inverse

def reference(patches, probe, w_key, w_value, w_out, texts):
    head_size = D // HEADS
    scaling = 1.0 / math.sqrt(head_size)
    query_table = head_table() * probe.astype(jnp.float32)[:, None]
    probe_keys = jnp.dot(w_key.astype(jnp.float32), query_table, precision=lax.Precision.HIGHEST)
    split_values = w_value.astype(jnp.float32).reshape(D, HEADS, head_size)
    image_groups = patches.reshape(N_GRP, GROUP, PATCH, D)
    text_groups = texts.reshape(N_GRP, GROUP, D)
    diagonal = jnp.eye(GROUP, dtype=jnp.float32)

    def one_group(pair):
        images, words = pair
        field = images.astype(jnp.float32)
        scores = jnp.einsum('rpd,dh->rph', field, probe_keys, precision=lax.Precision.HIGHEST) * scaling
        top = lax.optimization_barrier(jnp.max(scores, axis=1, keepdims=True))
        expo = jnp.exp(scores - top)
        weights = expo / lax.optimization_barrier(jnp.sum(expo, axis=1, keepdims=True))
        mixed = jnp.einsum('rph,rpd->rhd', weights, field, precision=lax.Precision.HIGHEST)
        pooled = jnp.einsum('rhd,dhk->rhk', mixed, split_values, precision=lax.Precision.HIGHEST)
        pooled = pooled.reshape(GROUP, D).astype(jnp.bfloat16)
        embed = jnp.dot(pooled, w_out, preferred_element_type=jnp.float32)
        unit_image, inverse_image = unit_rows(embed)
        unit_image_b = unit_image.astype(jnp.bfloat16)
        unit_text, inverse_text = unit_rows(words.astype(jnp.float32))
        unit_text_b = unit_text.astype(jnp.bfloat16)
        logits = 10.0 * lax.dot_general(unit_image_b, unit_text_b, (((1,), (1,)), ((), ())), preferred_element_type=jnp.float32) - 2.0
        slopes = (jax.nn.sigmoid(logits) - diagonal).astype(jnp.bfloat16)
        grad_unit_image = 10.0 * jnp.dot(slopes, unit_text_b, preferred_element_type=jnp.float32)
        grad_unit_text = 10.0 * lax.dot_general(slopes, unit_image_b, (((0,), (0,)), ((), ())), preferred_element_type=jnp.float32)
        return (chain_back(grad_unit_image, unit_image, inverse_image), chain_back(grad_unit_text, unit_text, inverse_text))
    grad_image, grad_text = lax.map(one_group, (image_groups, text_groups))
    return (grad_image.reshape(BATCH, D), grad_text.reshape(BATCH, D))
```

```python
import math

import jax
import jax.numpy as jnp
from jax import lax
from jax.experimental import pallas as pl
from jax.experimental.pallas import tpu as pltpu
from jax.sharding import PartitionSpec as P

HEADS = 16
MESH = pl.DeviceIdType.MESH
LANES = 128
F32 = jnp.float32
BF16 = jnp.bfloat16


def dot_rows(left, right):
    return lax.dot_general(left, right, (((1,), (1,)), ((), ())), preferred_element_type=F32)


def dot(left, right):
    return lax.dot_general(left, right, (((1,), (0,)), ((), ())), preferred_element_type=F32)


def unit_rows(values):
    inverse = lax.rsqrt(jnp.sum(values * values, axis=1, keepdims=True) + 1e-06)
    return values * inverse, inverse


def chain_back(grad_unit, unit_f, inverse):
    inner = jnp.sum(unit_f * grad_unit, axis=1, keepdims=True)
    return (grad_unit - unit_f * inner) * inverse


def slopes_of(logits, first_row):
    rows, columns = logits.shape
    row = lax.broadcasted_iota(jnp.int32, (rows, columns), 0) + first_row
    column = lax.broadcasted_iota(jnp.int32, (rows, columns), 1)
    target = jnp.where(row == column, 1.0, 0.0)
    return (jax.nn.sigmoid(10.0 * logits - 2.0) - target).astype(BF16)


def kernel(
    n_grp,
    n_blk,
    patches_hbm,
    probe_ref,
    w_key_hbm,
    w_value_hbm,
    w_out_hbm,
    texts_hbm,
    grad_image_ref,
    grad_text_ref,
    patches,
    w_key,
    w_value,
    w_out,
    texts,
    key_send,
    key_all,
    value_send,
    value_all,
    text_send,
    text_all,
    mixed_send,
    mixed_all,
    embed_send,
    embed_all,
    image_send,
    image_all,
    load_sem,
    send_sem,
    recv_sem,
):
    g, b = lax.axis_index("grp"), lax.axis_index("blk")
    rows = texts.shape[0]
    width = texts.shape[1]
    head_size = width // HEADS
    patch_count = patches.shape[0] // rows

    loads = {}
    for index, (name, source, target) in enumerate(
        (
            ("key", w_key_hbm, w_key),
            ("text", texts_hbm, texts),
            ("value", w_value_hbm, w_value),
            ("patches", patches_hbm, patches),
            ("out", w_out_hbm, w_out),
        )
    ):
        loads[name] = pltpu.make_async_copy(source, target, load_sem.at[index])
        loads[name].start()

    def grp_peer(step):
        return jnp.bitwise_xor(g, step)

    def blk_peer(step):
        return jnp.bitwise_xor(b, step)

    barrier = pltpu.get_barrier_semaphore()
    for step in range(1, n_grp):
        pl.semaphore_signal(barrier, inc=1, device_id=(grp_peer(step), b), device_id_type=MESH)
    for step in range(1, n_blk):
        pl.semaphore_signal(barrier, inc=1, device_id=(g, blk_peer(step)), device_id_type=MESH)

    def scatter(phase, source, target, axis, same):
        count = n_grp if axis == "grp" else n_blk
        for step in range(count - 1, 0, -1):
            peer = grp_peer(step) if axis == "grp" else blk_peer(step)
            device = (peer, b) if axis == "grp" else (g, peer)
            pltpu.make_async_remote_copy(
                src_ref=source if same else source.at[peer],
                dst_ref=target.at[g if axis == "grp" else b],
                send_sem=send_sem.at[phase],
                recv_sem=recv_sem.at[phase],
                device_id=device,
                device_id_type=MESH,
            ).start()

    def total_of(phase, target):
        many = target.at[pl.ds(0, target.shape[0] - 1)]
        return pltpu.make_async_remote_copy(
            src_ref=many,
            dst_ref=many,
            send_sem=send_sem.at[phase],
            recv_sem=recv_sem.at[phase],
            device_id=(g, b),
            device_id_type=MESH,
        )

    column = lax.broadcasted_iota(jnp.int32, (HEADS, width), 1)
    head = lax.broadcasted_iota(jnp.int32, (HEADS, width), 0)
    owned = (column >= head * head_size) & (column < (head + 1) * head_size)
    probe = jnp.broadcast_to(probe_ref[...].astype(F32), (HEADS, width))
    query_table = jnp.where(owned, probe, 0.0).astype(BF16)
    loads["key"].wait()
    keys = dot_rows(query_table, w_key[...])
    key_send[...] = jnp.zeros(key_send.shape, F32)
    key_send[:, :head_size] = keys
    key_all[pl.ds(g, 1)] = key_send[...][None]

    loads["text"].wait()
    unit_text, inverse_text = unit_rows(texts[...].astype(F32))
    text_send[...] = unit_text.astype(BF16)
    text_all[pl.ds(b, 1)] = text_send[...][None]

    loads["value"].wait()
    value_f = w_value[...].astype(F32)
    value_send[...] = jnp.zeros(value_send.shape, BF16)
    for h in range(HEADS):
        piece = value_f[:, h * head_size : (h + 1) * head_size]
        value_send[h, :head_size, :head_size] = piece.astype(BF16)
    value_all[pl.ds(g, 1)] = value_send[pl.ds(g, 1)]

    pl.semaphore_wait(barrier, n_grp + n_blk - 2)

    scatter(0, key_send, key_all, "grp", True)
    scatter(1, value_send, value_all, "grp", False)
    scatter(2, text_send, text_all, "blk", True)

    loads["patches"].wait()
    total_of(0, key_all).wait_recv()
    probe_keys = jnp.concatenate([key_all[i][:, :head_size] for i in range(n_grp)], axis=1)
    top_part = probe_keys.astype(BF16)
    rest = probe_keys - top_part.astype(F32)
    mid_part = rest.astype(BF16)
    low_part = (rest - mid_part.astype(F32)).astype(BF16)
    stacked = jnp.concatenate([top_part, mid_part, low_part], axis=0)
    parts = dot_rows(stacked, patches[...])
    scores = (parts[:HEADS] + parts[HEADS : 2 * HEADS] + parts[2 * HEADS :]) * (
        1.0 / math.sqrt(head_size)
    )
    flat = rows * patch_count
    spread = jnp.broadcast_to(scores[:, None, :], (HEADS, rows, flat)).reshape(HEADS * rows, flat)
    image = lax.broadcasted_iota(jnp.int32, (HEADS, rows, flat), 1).reshape(HEADS * rows, flat)
    position = lax.broadcasted_iota(jnp.int32, (HEADS * rows, flat), 1)
    inside = (position >= image * patch_count) & (position < (image + 1) * patch_count)
    spread = jnp.where(inside, spread, -jnp.inf)
    expo = jnp.exp(spread - jnp.max(spread, axis=1, keepdims=True)).astype(BF16)
    denominator = jnp.sum(expo.astype(F32), axis=1, keepdims=True)
    mixed = dot(expo, patches[...]) / denominator
    mixed_send[...] = mixed.reshape(HEADS, rows, width).astype(BF16)
    mixed_all[pl.ds(g, 1)] = mixed_send[pl.ds(g, 1)]
    scatter(3, mixed_send, mixed_all, "grp", False)

    total_of(1, value_all).wait_recv()
    value_head = value_all[...][:, :head_size, :].astype(F32).reshape(width, LANES).astype(BF16)
    loads["out"].wait()
    total_of(3, mixed_all).wait_recv()
    mixed_head = mixed_all[...].astype(F32).reshape(n_grp * rows, width).astype(BF16)
    pooled = dot(mixed_head, value_head)[:, :head_size].astype(BF16)
    partial_embed = dot(pooled, w_out[...])
    embed_send[...] = partial_embed.reshape(n_grp, rows, width).astype(BF16)
    embed_all[pl.ds(g, 1)] = embed_send[pl.ds(g, 1)]
    scatter(4, embed_send, embed_all, "grp", False)

    total_of(2, text_all).wait_recv()
    all_texts = text_all[...].astype(F32).reshape(n_blk * rows, width).astype(BF16)
    total_of(4, embed_all).wait_recv()
    embed = jnp.sum(embed_all[...].astype(F32), axis=0)
    unit_image, inverse_image = unit_rows(embed)
    unit_image_b = unit_image.astype(BF16)
    image_send[...] = unit_image_b
    image_all[pl.ds(b, 1)] = unit_image_b[None]
    scatter(5, image_send, image_all, "blk", True)

    slopes = slopes_of(dot_rows(unit_image_b, all_texts), b * rows)
    grad_image_ref[...] = chain_back(10.0 * dot(slopes, all_texts), unit_image, inverse_image)

    total_of(5, image_all).wait_recv()
    all_images = image_all[...].astype(F32).reshape(n_blk * rows, width).astype(BF16)
    slopes = slopes_of(dot_rows(text_send[...], all_images), b * rows)
    grad_text_ref[...] = chain_back(10.0 * dot(slopes, all_images), unit_text, inverse_text)

    for phase, target in enumerate((key_all, value_all, text_all, mixed_all, embed_all, image_all)):
        total_of(phase, target).wait_send()


def solution(mesh):
    n_grp, n_blk = mesh.shape["grp"], mesh.shape["blk"]

    def local(patches, probe, w_key, w_value, w_out, texts):
        rows, patch_count, width = patches.shape
        depth = w_key.shape[0]
        padded = -(-depth // 16) * 16
        hbm = pl.BlockSpec(memory_space=pltpu.HBM)
        vmem = pl.BlockSpec(memory_space=pltpu.VMEM)
        out = jax.ShapeDtypeStruct((rows, width), F32)
        return pl.pallas_call(
            lambda *refs: kernel(n_grp, n_blk, *refs),
            out_shape=(out, out),
            in_specs=[hbm, vmem, hbm, hbm, hbm, hbm],
            out_specs=(vmem, vmem),
            scratch_shapes=[
                pltpu.VMEM((rows * patch_count, width), BF16),
                pltpu.VMEM((depth, width), BF16),
                pltpu.VMEM((depth, width), BF16),
                pltpu.VMEM((depth, width), BF16),
                pltpu.VMEM((rows, width), BF16),
                pltpu.VMEM((HEADS, LANES), F32),
                pltpu.VMEM((n_grp, HEADS, LANES), F32),
                pltpu.VMEM((n_grp, padded, LANES), BF16),
                pltpu.VMEM((n_grp, padded, LANES), BF16),
                pltpu.VMEM((rows, width), BF16),
                pltpu.VMEM((n_blk, rows, width), BF16),
                pltpu.VMEM((n_grp, rows, width), BF16),
                pltpu.VMEM((n_grp, rows, width), BF16),
                pltpu.VMEM((n_grp, rows, width), BF16),
                pltpu.VMEM((n_grp, rows, width), BF16),
                pltpu.VMEM((rows, width), BF16),
                pltpu.VMEM((n_blk, rows, width), BF16),
                pltpu.SemaphoreType.DMA((5,)),
                pltpu.SemaphoreType.DMA((6,)),
                pltpu.SemaphoreType.DMA((6,)),
            ],
            compiler_params=pltpu.CompilerParams(
                collective_id=0, has_side_effects=True, vmem_limit_bytes=56 << 20
            ),
        )(patches.reshape(rows * patch_count, width), probe.reshape(1, width), w_key, w_value, w_out, texts)

    split = P(("grp", "blk"), None)
    in_specs = (P(("grp", "blk"), None, None), P(), P("grp", None), P("grp", None), P("grp", None), split)
    return jax.shard_map(local, mesh=mesh, in_specs=in_specs, out_specs=(split, split), check_vma=False)
```

```python
import math

import jax
import jax.numpy as jnp
from jax import lax
from jax.experimental import pallas as pl
from jax.experimental.pallas import tpu as pltpu
from jax.sharding import PartitionSpec as P

HEADS = 16
MESH = pl.DeviceIdType.MESH
LANES = 128
F32 = jnp.float32
BF16 = jnp.bfloat16


def dot_rows(left, right):
    return lax.dot_general(left, right, (((1,), (1,)), ((), ())), preferred_element_type=F32)


def dot(left, right):
    return lax.dot_general(left, right, (((1,), (0,)), ((), ())), preferred_element_type=F32)


def unit_rows(values):
    inverse = lax.rsqrt(jnp.sum(values * values, axis=1, keepdims=True) + 1e-06)
    return values * inverse, inverse


def chain_back(grad_unit, unit_f, inverse):
    inner = jnp.sum(unit_f * grad_unit, axis=1, keepdims=True)
    return (grad_unit - unit_f * inner) * inverse


def slopes_of(logits, first_row):
    rows, columns = logits.shape
    row = lax.broadcasted_iota(jnp.int32, (rows, columns), 0) + first_row
    column = lax.broadcasted_iota(jnp.int32, (rows, columns), 1)
    target = jnp.where(row == column, 1.0, 0.0)
    return (jax.nn.sigmoid(10.0 * logits - 2.0) - target).astype(BF16)


def kernel(
    n_grp,
    n_blk,
    patches_hbm,
    probe_hbm,
    w_key_hbm,
    w_value_hbm,
    w_out_hbm,
    texts_hbm,
    grads_ref,
    patches,
    probe_local,
    w_key,
    w_value,
    w_out,
    texts,
    key_send,
    key_all,
    value_send,
    value_all,
    text_send,
    text_all,
    mixed_send,
    mixed_all,
    embed_send,
    embed_all,
    image_send,
    image_all,
    load_sem,
    send_sem,
    recv_sem,
):
    g, b = lax.axis_index("grp"), lax.axis_index("blk")
    rows = texts.shape[0]
    width = texts.shape[1]
    head_size = width // HEADS
    patch_count = patches.shape[0] // rows

    loads = {}
    for index, (name, source, target) in enumerate(
        (
            ("probe", probe_hbm, probe_local),
            ("key", w_key_hbm, w_key),
            ("text", texts_hbm, texts),
            ("value", w_value_hbm, w_value),
            ("patches", patches_hbm, patches),
            ("out", w_out_hbm, w_out),
        )
    ):
        loads[name] = pltpu.make_async_copy(source, target, load_sem.at[index])
        loads[name].start()

    def grp_peer(step):
        return jnp.bitwise_xor(g, step)

    def blk_peer(step):
        return jnp.bitwise_xor(b, step)

    barrier = pltpu.get_barrier_semaphore()
    for step in range(1, n_grp):
        pl.semaphore_signal(barrier, inc=1, device_id=(grp_peer(step), b), device_id_type=MESH)
    for step in range(1, n_blk):
        pl.semaphore_signal(barrier, inc=1, device_id=(g, blk_peer(step)), device_id_type=MESH)

    def scatter(phase, source, target, axis, same):
        count = n_grp if axis == "grp" else n_blk
        for step in range(count - 1, 0, -1):
            peer = grp_peer(step) if axis == "grp" else blk_peer(step)
            device = (peer, b) if axis == "grp" else (g, peer)
            pltpu.make_async_remote_copy(
                src_ref=source if same else source.at[peer],
                dst_ref=target.at[g if axis == "grp" else b],
                send_sem=send_sem.at[phase],
                recv_sem=recv_sem.at[phase],
                device_id=device,
                device_id_type=MESH,
            ).start()

    def total_of(phase, target):
        many = target.at[pl.ds(0, target.shape[0] - 1)]
        return pltpu.make_async_remote_copy(
            src_ref=many,
            dst_ref=many,
            send_sem=send_sem.at[phase],
            recv_sem=recv_sem.at[phase],
            device_id=(g, b),
            device_id_type=MESH,
        )

    column = lax.broadcasted_iota(jnp.int32, (HEADS, width), 1)
    head = lax.broadcasted_iota(jnp.int32, (HEADS, width), 0)
    owned = (column >= head * head_size) & (column < (head + 1) * head_size)
    loads["probe"].wait()
    probe = jnp.broadcast_to(probe_local[...].astype(F32)[None, :], (HEADS, width))
    query_table = jnp.where(owned, probe, 0.0).astype(BF16)
    loads["key"].wait()
    keys = dot_rows(query_table, w_key[...])
    key_send[...] = jnp.zeros(key_send.shape, F32)
    key_send[:, :head_size] = keys
    key_all[pl.ds(g, 1)] = key_send[...][None]

    loads["text"].wait()
    unit_text, inverse_text = unit_rows(texts[...].astype(F32))
    text_send[...] = unit_text.astype(BF16)
    text_all[pl.ds(b, 1)] = text_send[...][None]

    loads["value"].wait()
    value_f = w_value[...].astype(F32)
    value_send[...] = jnp.zeros(value_send.shape, BF16)
    for h in range(HEADS):
        piece = value_f[:, h * head_size : (h + 1) * head_size]
        value_send[h, :head_size, :head_size] = piece.astype(BF16)
    value_all[pl.ds(g, 1)] = value_send[pl.ds(g, 1)]

    pl.semaphore_wait(barrier, n_grp + n_blk - 2)

    scatter(0, key_send, key_all, "grp", True)
    scatter(1, value_send, value_all, "grp", False)
    scatter(2, text_send, text_all, "blk", True)

    loads["patches"].wait()
    total_of(0, key_all).wait_recv()
    probe_keys = jnp.concatenate([key_all[i][:, :head_size] for i in range(n_grp)], axis=1)
    top_part = probe_keys.astype(BF16)
    rest = probe_keys - top_part.astype(F32)
    mid_part = rest.astype(BF16)
    low_part = (rest - mid_part.astype(F32)).astype(BF16)
    stacked = jnp.concatenate([top_part, mid_part, low_part], axis=0)
    parts = dot_rows(stacked, patches[...])
    scores = (parts[:HEADS] + parts[HEADS : 2 * HEADS] + parts[2 * HEADS :]) * (
        1.0 / math.sqrt(head_size)
    )
    flat = rows * patch_count
    spread = jnp.broadcast_to(scores[:, None, :], (HEADS, rows, flat)).reshape(HEADS * rows, flat)
    image = lax.broadcasted_iota(jnp.int32, (HEADS, rows, flat), 1).reshape(HEADS * rows, flat)
    position = lax.broadcasted_iota(jnp.int32, (HEADS * rows, flat), 1)
    inside = (position >= image * patch_count) & (position < (image + 1) * patch_count)
    spread = jnp.where(inside, spread, -jnp.inf)
    expo = jnp.exp(spread - jnp.max(spread, axis=1, keepdims=True)).astype(BF16)
    denominator = jnp.sum(expo.astype(F32), axis=1, keepdims=True)
    mixed = dot(expo, patches[...]) / denominator
    mixed_send[...] = mixed.reshape(HEADS, rows, width).astype(BF16)
    mixed_all[pl.ds(g, 1)] = mixed_send[pl.ds(g, 1)]
    scatter(3, mixed_send, mixed_all, "grp", False)

    total_of(1, value_all).wait_recv()
    value_head = value_all[...][:, :head_size, :].astype(F32).reshape(width, LANES).astype(BF16)
    loads["out"].wait()
    total_of(3, mixed_all).wait_recv()
    mixed_head = mixed_all[...].astype(F32).reshape(n_grp * rows, width).astype(BF16)
    pooled = dot(mixed_head, value_head)[:, :head_size].astype(BF16)
    partial_embed = dot(pooled, w_out[...])
    embed_send[...] = partial_embed.reshape(n_grp, rows, width).astype(BF16)
    embed_all[pl.ds(g, 1)] = embed_send[pl.ds(g, 1)]
    scatter(4, embed_send, embed_all, "grp", False)

    total_of(2, text_all).wait_recv()
    all_texts = text_all[...].astype(F32).reshape(n_blk * rows, width).astype(BF16)
    total_of(4, embed_all).wait_recv()
    embed = jnp.sum(embed_all[...].astype(F32), axis=0)
    unit_image, inverse_image = unit_rows(embed)
    unit_image_b = unit_image.astype(BF16)
    image_send[...] = unit_image_b
    image_all[pl.ds(b, 1)] = unit_image_b[None]
    scatter(5, image_send, image_all, "blk", True)

    slopes = slopes_of(dot_rows(unit_image_b, all_texts), b * rows)
    grads_ref[:rows] = chain_back(10.0 * dot(slopes, all_texts), unit_image, inverse_image)

    total_of(5, image_all).wait_recv()
    all_images = image_all[...].astype(F32).reshape(n_blk * rows, width).astype(BF16)
    slopes = slopes_of(dot_rows(text_send[...], all_images), b * rows)
    grads_ref[rows:] = chain_back(10.0 * dot(slopes, all_images), unit_text, inverse_text)

    for phase, target in enumerate((key_all, value_all, text_all, mixed_all, embed_all, image_all)):
        total_of(phase, target).wait_send()


def solution(mesh):
    n_grp, n_blk = mesh.shape["grp"], mesh.shape["blk"]

    def local(patches, probe, w_key, w_value, w_out, texts):
        rows, patch_count, width = patches.shape
        depth = w_key.shape[0]
        padded = -(-depth // 16) * 16
        hbm = pl.BlockSpec(memory_space=pltpu.HBM)
        vmem = pl.BlockSpec(memory_space=pltpu.VMEM)
        operands = (patches.reshape(rows * patch_count, width), probe, w_key, w_value, w_out, texts)
        grads = pl.pallas_call(
            lambda *refs: kernel(n_grp, n_blk, *refs),
            out_shape=pltpu.VMEM((2 * rows, width), F32),
            in_specs=[hbm] * len(operands),
            out_specs=vmem,
            scratch_shapes=[
                pltpu.VMEM((rows * patch_count, width), BF16),
                pltpu.VMEM((width,), BF16),
                pltpu.VMEM((depth, width), BF16),
                pltpu.VMEM((depth, width), BF16),
                pltpu.VMEM((depth, width), BF16),
                pltpu.VMEM((rows, width), BF16),
                pltpu.VMEM((HEADS, LANES), F32),
                pltpu.VMEM((n_grp, HEADS, LANES), F32),
                pltpu.VMEM((n_grp, padded, LANES), BF16),
                pltpu.VMEM((n_grp, padded, LANES), BF16),
                pltpu.VMEM((rows, width), BF16),
                pltpu.VMEM((n_blk, rows, width), BF16),
                pltpu.VMEM((n_grp, rows, width), BF16),
                pltpu.VMEM((n_grp, rows, width), BF16),
                pltpu.VMEM((n_grp, rows, width), BF16),
                pltpu.VMEM((n_grp, rows, width), BF16),
                pltpu.VMEM((rows, width), BF16),
                pltpu.VMEM((n_blk, rows, width), BF16),
                pltpu.SemaphoreType.DMA((6,)),
                pltpu.SemaphoreType.DMA((6,)),
                pltpu.SemaphoreType.DMA((6,)),
            ],
            compiler_params=pltpu.CompilerParams(
                collective_id=0, has_side_effects=True, vmem_limit_bytes=24 << 20
            ),
        )(*(pltpu.with_memory_space_constraint(x, pltpu.HBM) for x in operands))
        return grads[:rows], grads[rows:]

    split = P(("grp", "blk"), None)
    in_specs = (P(("grp", "blk"), None, None), P(), P("grp", None), P("grp", None), P("grp", None), split)
    return jax.shard_map(local, mesh=mesh, in_specs=in_specs, out_specs=(split, split), check_vma=False)
```

```python
import math

import jax
import jax.numpy as jnp
from jax import lax
from jax.experimental import pallas as pl
from jax.experimental.pallas import tpu as pltpu
from jax.sharding import PartitionSpec as P

HEADS = 16
MESH = pl.DeviceIdType.MESH
LANES = 128
F32 = jnp.float32
BF16 = jnp.bfloat16
GRP_STEPS = (11, 15, 7, 10, 14, 6, 9, 13, 5, 8, 12, 4, 3, 2, 1)
Z_STEPS = (4, 3, 5, 2, 6, 1, 7)
KEYS, VALUES, TEXT_ONE, TEXT_PAIRS, MIXED, EMBED, IMAGE = 0, 1, 2, 3, 4, 5, 6
PHASES = 7


def dot_rows(left, right):
    return lax.dot_general(left, right, (((1,), (1,)), ((), ())), preferred_element_type=F32)


def dot(left, right):
    return lax.dot_general(left, right, (((1,), (0,)), ((), ())), preferred_element_type=F32)


def unit_rows(values):
    inverse = lax.rsqrt(jnp.sum(values * values, axis=1, keepdims=True) + 1e-06)
    return values * inverse, inverse


def chain_back(grad_unit, unit_f, inverse):
    inner = jnp.sum(unit_f * grad_unit, axis=1, keepdims=True)
    return (grad_unit - unit_f * inner) * inverse


def slopes_of(logits, first_row):
    rows, columns = logits.shape
    row = lax.broadcasted_iota(jnp.int32, (rows, columns), 0) + first_row
    column = lax.broadcasted_iota(jnp.int32, (rows, columns), 1)
    target = jnp.where(row == column, 1.0, 0.0)
    return (jax.nn.sigmoid(10.0 * logits - 2.0) - target).astype(BF16)


def pack_block(block):
    size = block.shape[1]
    low, room = 2 * size // 3, LANES - size
    rest = block[low:]
    blank = jnp.zeros((size - low, 2 * room - size), F32)
    over = jnp.concatenate([rest[:, room:], blank], axis=1)
    right = jnp.concatenate([rest[:, :room], over], axis=0)
    return jnp.concatenate([block[:low], right], axis=1)


def unpack_block(packed, size):
    half, room = size // 3, LANES - size
    rest = jnp.concatenate([packed[:half, size:], packed[half:, size : 2 * size - room]], axis=1)
    return jnp.concatenate([packed[:, :size], rest], axis=0)


def kernel(
    n_grp,
    n_blk,
    patches_hbm,
    probe_hbm,
    w_key_hbm,
    w_value_hbm,
    w_out_hbm,
    texts_hbm,
    grads_ref,
    patches,
    probe_local,
    w_key,
    w_value,
    w_out,
    texts,
    key_send,
    key_all,
    value_send,
    value_all,
    text_all,
    mixed_send,
    mixed_all,
    embed_send,
    embed_all,
    image_send,
    image_all,
    load_sem,
    send_sem,
    recv_sem,
):
    g, b = lax.axis_index("grp"), lax.axis_index("blk")
    rows = texts.shape[0]
    width = texts.shape[1]
    head_size = width // HEADS
    patch_count = patches.shape[0] // rows
    n_z = n_blk // 2
    z, x_hi = lax.rem(b, n_z), lax.div(b, n_z)
    first_text = (z * 2 + x_hi) * rows

    loads = {}
    for index, (name, source, target) in enumerate(
        (
            ("probe", probe_hbm, probe_local),
            ("key", w_key_hbm, w_key),
            ("text", texts_hbm, texts),
            ("value", w_value_hbm, w_value),
            ("patches", patches_hbm, patches),
            ("out", w_out_hbm, w_out),
        )
    ):
        loads[name] = pltpu.make_async_copy(source, target, load_sem.at[index])
        loads[name].start()

    def grp_peer(step):
        return (jnp.bitwise_xor(g, step), b)

    def blk_peer(turn, step):
        return (g, lax.rem(x_hi + turn, 2) * n_z + lax.rem(z + step, n_z))

    barrier = pltpu.get_barrier_semaphore()
    for step in GRP_STEPS:
        pl.semaphore_signal(barrier, inc=1, device_id=grp_peer(step), device_id_type=MESH)
    blk_peers = [blk_peer(1, step) for step in Z_STEPS + (0,)] + [blk_peer(0, step) for step in Z_STEPS]
    for peer in blk_peers:
        pl.semaphore_signal(barrier, inc=1, device_id=peer, device_id_type=MESH)

    def copy(phase, source, target, device):
        return pltpu.make_async_remote_copy(
            src_ref=source,
            dst_ref=target,
            send_sem=send_sem.at[phase],
            recv_sem=recv_sem.at[phase],
            device_id=device,
            device_id_type=MESH,
        )

    def total_of(phase):
        many = {
            KEYS: key_all.at[pl.ds(0, n_grp - 1)],
            VALUES: value_all.at[pl.ds(0, n_grp - 1)],
            TEXT_ONE: text_all.at[0, 0],
            TEXT_PAIRS: text_all.at[pl.ds(0, n_z - 1)],
            MIXED: mixed_all.at[pl.ds(0, n_grp - 1)],
            EMBED: embed_all.at[pl.ds(0, n_grp - 1)],
            IMAGE: image_all.at[pl.ds(0, n_blk - 1)],
        }[phase]
        return copy(phase, many, many, (g, b))

    column = lax.broadcasted_iota(jnp.int32, (HEADS, width), 1)
    head = lax.broadcasted_iota(jnp.int32, (HEADS, width), 0)
    owned = (column >= head * head_size) & (column < (head + 1) * head_size)
    loads["probe"].wait()
    probe = jnp.broadcast_to(probe_local[...].astype(F32)[None, :], (HEADS, width))
    query_table = jnp.where(owned, probe, 0.0).astype(BF16)
    loads["key"].wait()
    keys = dot_rows(query_table, w_key[...])
    key_send[...] = jnp.zeros(key_send.shape, F32)
    key_send[:, :head_size] = keys
    key_all[pl.ds(g, 1)] = key_send[...][None]

    loads["text"].wait()
    unit_text, inverse_text = unit_rows(texts[...].astype(F32))
    unit_text_b = unit_text.astype(BF16)
    text_all[pl.ds(z, 1), pl.ds(x_hi, 1)] = unit_text_b[None, None]

    pl.semaphore_wait(barrier, n_grp + n_blk - 2)
    for step in GRP_STEPS:
        copy(KEYS, key_send, key_all.at[g], grp_peer(step)).start()
    copy(TEXT_ONE, text_all.at[z, x_hi], text_all.at[z, x_hi], blk_peer(1, 0)).start()

    loads["value"].wait()
    value_f = w_value[...].astype(F32)
    for h in range(HEADS):
        value_send[h] = pack_block(value_f[:, h * head_size : (h + 1) * head_size]).astype(BF16)
    value_all[pl.ds(g, 1)] = value_send[pl.ds(g, 1)]
    for step in GRP_STEPS:
        peer = grp_peer(step)
        copy(VALUES, value_send.at[peer[0]], value_all.at[g], peer).start()

    loads["patches"].wait()
    total_of(KEYS).wait_recv()
    probe_keys = jnp.concatenate([key_all[i][:, :head_size] for i in range(n_grp)], axis=1)
    top_part = probe_keys.astype(BF16)
    rest = probe_keys - top_part.astype(F32)
    mid_part = rest.astype(BF16)
    low_part = (rest - mid_part.astype(F32)).astype(BF16)
    stacked = jnp.concatenate([top_part, mid_part, low_part], axis=0)
    parts = dot_rows(stacked, patches[...])
    scores = (parts[:HEADS] + parts[HEADS : 2 * HEADS] + parts[2 * HEADS :]) * (
        1.0 / math.sqrt(head_size)
    )
    flat = rows * patch_count
    spread = jnp.broadcast_to(scores[:, None, :], (HEADS, rows, flat)).reshape(HEADS * rows, flat)
    image = lax.broadcasted_iota(jnp.int32, (HEADS, rows, flat), 1).reshape(HEADS * rows, flat)
    position = lax.broadcasted_iota(jnp.int32, (HEADS * rows, flat), 1)
    inside = (position >= image * patch_count) & (position < (image + 1) * patch_count)
    spread = jnp.where(inside, spread, -jnp.inf)
    expo = jnp.exp(spread - jnp.max(spread, axis=1, keepdims=True)).astype(BF16)
    denominator = jnp.sum(expo.astype(F32), axis=1, keepdims=True)
    mixed = dot(expo, patches[...]) / denominator
    mixed_send[...] = mixed.reshape(HEADS, rows, width).astype(BF16)
    mixed_all[pl.ds(g, 1)] = mixed_send[pl.ds(g, 1)]
    for step in GRP_STEPS:
        peer = grp_peer(step)
        copy(MIXED, mixed_send.at[peer[0]], mixed_all.at[g], peer).start()

    total_of(TEXT_ONE).wait_recv()
    for step in Z_STEPS:
        copy(TEXT_PAIRS, text_all.at[z], text_all.at[z], blk_peer(0, step)).start()

    total_of(VALUES).wait_recv()
    value_head = jnp.concatenate(
        [unpack_block(value_all[i].astype(F32), head_size) for i in range(n_grp)], axis=0
    ).astype(BF16)
    loads["out"].wait()
    total_of(MIXED).wait_recv()
    mixed_head = mixed_all[...].astype(F32).reshape(n_grp * rows, width).astype(BF16)
    pooled = dot(mixed_head, value_head).astype(BF16)
    partial_embed = dot(pooled, w_out[...])
    embed_send[...] = partial_embed.reshape(n_grp, rows, width).astype(BF16)
    embed_all[pl.ds(g, 1)] = embed_send[pl.ds(g, 1)]
    for step in GRP_STEPS:
        peer = grp_peer(step)
        copy(EMBED, embed_send.at[peer[0]], embed_all.at[g], peer).start()

    total_of(TEXT_PAIRS).wait_recv()
    all_texts = text_all[...].astype(F32).reshape(n_blk * rows, width).astype(BF16)
    total_of(EMBED).wait_recv()
    unit_image, inverse_image = unit_rows(jnp.sum(embed_all[...].astype(F32), axis=0))
    unit_image_b = unit_image.astype(BF16)
    image_send[...] = unit_image_b
    image_all[pl.ds(b, 1)] = unit_image_b[None]
    for peer in [(g, jnp.bitwise_xor(b, k)) for k in range(15, 0, -1)]:
        copy(IMAGE, image_send, image_all.at[b], peer).start()

    slopes = slopes_of(dot_rows(unit_image_b, all_texts), first_text)
    grads_ref[:rows] = chain_back(10.0 * dot(slopes, all_texts), unit_image, inverse_image)

    total_of(IMAGE).wait_recv()
    all_images = image_all[...].astype(F32).reshape(n_blk * rows, width).astype(BF16)
    slopes = slopes_of(dot_rows(unit_text_b, all_images), b * rows)
    grads_ref[rows:] = chain_back(10.0 * dot(slopes, all_images), unit_text, inverse_text)

    for phase in range(PHASES):
        total_of(phase).wait_send()


def solution(mesh):
    n_grp, n_blk = mesh.shape["grp"], mesh.shape["blk"]

    def local(patches, probe, w_key, w_value, w_out, texts):
        rows, patch_count, width = patches.shape
        depth = w_key.shape[0]
        packed = 2 * depth // 3
        hbm = pl.BlockSpec(memory_space=pltpu.HBM)
        vmem = pl.BlockSpec(memory_space=pltpu.VMEM)
        operands = (patches.reshape(rows * patch_count, width), probe, w_key, w_value, w_out, texts)
        grads = pl.pallas_call(
            lambda *refs: kernel(n_grp, n_blk, *refs),
            out_shape=pltpu.VMEM((2 * rows, width), F32),
            in_specs=[hbm] * len(operands),
            out_specs=vmem,
            scratch_shapes=[
                pltpu.VMEM((rows * patch_count, width), BF16),
                pltpu.VMEM((width,), BF16),
                pltpu.VMEM((depth, width), BF16),
                pltpu.VMEM((depth, width), BF16),
                pltpu.VMEM((depth, width), BF16),
                pltpu.VMEM((rows, width), BF16),
                pltpu.VMEM((HEADS, LANES), F32),
                pltpu.VMEM((n_grp, HEADS, LANES), F32),
                pltpu.VMEM((n_grp, packed, LANES), BF16),
                pltpu.VMEM((n_grp, packed, LANES), BF16),
                pltpu.VMEM((n_blk // 2, 2, rows, width), BF16),
                pltpu.VMEM((n_grp, rows, width), BF16),
                pltpu.VMEM((n_grp, rows, width), BF16),
                pltpu.VMEM((n_grp, rows, width), BF16),
                pltpu.VMEM((n_grp, rows, width), BF16),
                pltpu.VMEM((rows, width), BF16),
                pltpu.VMEM((n_blk, rows, width), BF16),
                pltpu.SemaphoreType.DMA((6,)),
                pltpu.SemaphoreType.DMA((PHASES,)),
                pltpu.SemaphoreType.DMA((PHASES,)),
            ],
            compiler_params=pltpu.CompilerParams(
                collective_id=0, has_side_effects=True, vmem_limit_bytes=24 << 20
            ),
        )(*(pltpu.with_memory_space_constraint(x, pltpu.HBM) for x in operands))
        return grads[:rows], grads[rows:]

    split = P(("grp", "blk"), None)
    in_specs = (P(("grp", "blk"), None, None), P(), P("grp", None), P("grp", None), P("grp", None), split)
    return jax.shard_map(local, mesh=mesh, in_specs=in_specs, out_specs=(split, split), check_vma=False)
```

```python
import math

import jax
import jax.numpy as jnp
from jax import lax
from jax.experimental import pallas as pl
from jax.experimental.pallas import tpu as pltpu
from jax.sharding import PartitionSpec as P

HEADS = 16
MESH = pl.DeviceIdType.MESH
LANES = 128
F32 = jnp.float32
BF16 = jnp.bfloat16
GRP_STEPS = (11, 15, 7, 10, 14, 6, 9, 13, 5, 8, 12, 4, 3, 2, 1)
Z_STEPS = (4, 3, 5, 2, 6, 1, 7)
BLK_ORDER = (0, 1, 2, 8, 3, 9, 10, 11, 4, 7, 5, 6, 12, 15, 13, 14)
BLK_ORDER_ODD = (0, 8, 1, 9, 2, 10, 3, 11, 4, 7, 5, 6, 12, 15, 13, 14)
KEYS, VALUES, TEXT_ONE, TEXT_PAIRS, MIXED, EMBED, IMAGE = 0, 1, 2, 3, 4, 5, 6
PHASES = 7


def dot_rows(left, right):
    return lax.dot_general(left, right, (((1,), (1,)), ((), ())), preferred_element_type=F32)


def dot(left, right):
    return lax.dot_general(left, right, (((1,), (0,)), ((), ())), preferred_element_type=F32)


def unit_rows(values):
    inverse = lax.rsqrt(jnp.sum(values * values, axis=1, keepdims=True) + 1e-06)
    return values * inverse, inverse


def chain_back(grad_unit, unit_f, inverse):
    inner = jnp.sum(unit_f * grad_unit, axis=1, keepdims=True)
    return (grad_unit - unit_f * inner) * inverse


def slopes_of(logits, first_row):
    rows, columns = logits.shape
    row = lax.broadcasted_iota(jnp.int32, (rows, columns), 0) + first_row
    column = lax.broadcasted_iota(jnp.int32, (rows, columns), 1)
    target = jnp.where(row == column, 1.0, 0.0)
    return (jax.nn.sigmoid(10.0 * logits - 2.0) - target).astype(BF16)


def pack_block(block):
    size = block.shape[1]
    low, room = 2 * size // 3, LANES - size
    rest = block[low:]
    blank = jnp.zeros((size - low, 2 * room - size), F32)
    over = jnp.concatenate([rest[:, room:], blank], axis=1)
    right = jnp.concatenate([rest[:, :room], over], axis=0)
    return jnp.concatenate([block[:low], right], axis=1)


def unpack_block(packed, size):
    half, room = size // 3, LANES - size
    rest = jnp.concatenate([packed[:half, size:], packed[half:, size : 2 * size - room]], axis=1)
    return jnp.concatenate([packed[:, :size], rest], axis=0)


def kernel(
    n_grp,
    n_blk,
    patches_hbm,
    probe_hbm,
    w_key_hbm,
    w_value_hbm,
    w_out_hbm,
    texts_hbm,
    grads_ref,
    patches,
    probe_local,
    w_key,
    w_value,
    w_out,
    texts,
    key_send,
    key_all,
    value_send,
    value_all,
    text_all,
    mixed_send,
    mixed_all,
    embed_send,
    embed_all,
    image_send,
    image_all,
    load_sem,
    send_sem,
    recv_sem,
):
    g, b = lax.axis_index("grp"), lax.axis_index("blk")
    rows = texts.shape[0]
    width = texts.shape[1]
    head_size = width // HEADS
    patch_count = patches.shape[0] // rows
    n_z = n_blk // 2
    z, x_hi = lax.rem(b, n_z), lax.div(b, n_z)
    first_text = (z * 2 + x_hi) * rows

    def grp_peer(step):
        return (jnp.bitwise_xor(g, step), b)

    def blk_peer(turn, step):
        return (g, lax.rem(x_hi + turn, 2) * n_z + lax.rem(z + step, n_z))

    barrier = pltpu.get_barrier_semaphore()
    for step in GRP_STEPS:
        pl.semaphore_signal(barrier, inc=1, device_id=grp_peer(step), device_id_type=MESH)
    blk_peers = [blk_peer(1, step) for step in Z_STEPS + (0,)] + [blk_peer(0, step) for step in Z_STEPS]
    for peer in blk_peers:
        pl.semaphore_signal(barrier, inc=1, device_id=peer, device_id_type=MESH)

    loads = {}
    for index, (name, source, target) in enumerate(
        (
            ("probe", probe_hbm, probe_local),
            ("key", w_key_hbm, w_key),
            ("text", texts_hbm, texts),
            ("value", w_value_hbm, w_value),
            ("patches", patches_hbm, patches),
            ("out", w_out_hbm, w_out),
        )
    ):
        loads[name] = pltpu.make_async_copy(source, target, load_sem.at[index])
        loads[name].start()

    def copy(phase, source, target, device):
        return pltpu.make_async_remote_copy(
            src_ref=source,
            dst_ref=target,
            send_sem=send_sem.at[phase],
            recv_sem=recv_sem.at[phase],
            device_id=device,
            device_id_type=MESH,
        )

    def total_of(phase):
        many = {
            KEYS: key_all.at[pl.ds(0, n_grp - 1)],
            VALUES: value_all.at[pl.ds(0, n_grp - 1)],
            TEXT_ONE: text_all.at[0, 0],
            TEXT_PAIRS: text_all.at[pl.ds(0, n_z - 1)],
            MIXED: mixed_all.at[pl.ds(0, n_grp - 1)],
            EMBED: embed_all.at[pl.ds(0, n_grp - 1)],
            IMAGE: image_all.at[pl.ds(0, n_blk - 1)],
        }[phase]
        return copy(phase, many, many, (g, b))

    column = lax.broadcasted_iota(jnp.int32, (HEADS, width), 1)
    head = lax.broadcasted_iota(jnp.int32, (HEADS, width), 0)
    owned = (column >= head * head_size) & (column < (head + 1) * head_size)
    loads["probe"].wait()
    probe = jnp.broadcast_to(probe_local[...].astype(F32)[None, :], (HEADS, width))
    query_table = jnp.where(owned, probe, 0.0).astype(BF16)
    loads["key"].wait()
    keys = dot_rows(query_table, w_key[...])
    key_send[...] = jnp.zeros(key_send.shape, F32)
    key_send[:, :head_size] = keys
    key_all[pl.ds(g, 1)] = key_send[...][None]

    loads["text"].wait()
    unit_text, inverse_text = unit_rows(texts[...].astype(F32))
    unit_text_b = unit_text.astype(BF16)
    text_all[pl.ds(z, 1), pl.ds(x_hi, 1)] = unit_text_b[None, None]

    pl.semaphore_wait(barrier, n_grp + n_blk - 2)
    for step in GRP_STEPS:
        copy(KEYS, key_send, key_all.at[g], grp_peer(step)).start()
    copy(TEXT_ONE, text_all.at[z, x_hi], text_all.at[z, x_hi], blk_peer(1, 0)).start()

    loads["value"].wait()
    value_f = w_value[...].astype(F32)
    for h in range(HEADS):
        value_send[h] = pack_block(value_f[:, h * head_size : (h + 1) * head_size]).astype(BF16)
    value_all[pl.ds(g, 1)] = value_send[pl.ds(g, 1)]
    for step in GRP_STEPS:
        peer = grp_peer(step)
        copy(VALUES, value_send.at[peer[0]], value_all.at[g], peer).start()

    loads["patches"].wait()
    total_of(KEYS).wait_recv()
    total_of(TEXT_ONE).wait_recv()
    for step in Z_STEPS:
        copy(TEXT_PAIRS, text_all.at[z], text_all.at[z], blk_peer(0, step)).start()
    probe_keys = jnp.concatenate([key_all[i][:, :head_size] for i in range(n_grp)], axis=1)
    top_part = probe_keys.astype(BF16)
    rest = probe_keys - top_part.astype(F32)
    mid_part = rest.astype(BF16)
    low_part = (rest - mid_part.astype(F32)).astype(BF16)
    stacked = jnp.concatenate([top_part, mid_part, low_part], axis=0)
    parts = dot_rows(stacked, patches[...])
    scores = (parts[:HEADS] + parts[HEADS : 2 * HEADS] + parts[2 * HEADS :]) * (
        1.0 / math.sqrt(head_size)
    )
    flat = rows * patch_count
    spread = jnp.broadcast_to(scores[:, None, :], (HEADS, rows, flat)).reshape(HEADS * rows, flat)
    image = lax.broadcasted_iota(jnp.int32, (HEADS, rows, flat), 1).reshape(HEADS * rows, flat)
    position = lax.broadcasted_iota(jnp.int32, (HEADS * rows, flat), 1)
    inside = (position >= image * patch_count) & (position < (image + 1) * patch_count)
    spread = jnp.where(inside, spread, -jnp.inf)
    expo = jnp.exp(spread - jnp.max(spread, axis=1, keepdims=True)).astype(BF16)
    denominator = jnp.sum(expo.astype(F32), axis=1, keepdims=True)
    mixed = dot(expo, patches[...]) / denominator
    mixed_send[...] = mixed.reshape(HEADS, rows, width).astype(BF16)
    mixed_all[pl.ds(g, 1)] = mixed_send[pl.ds(g, 1)]
    for step in GRP_STEPS:
        peer = grp_peer(step)
        copy(MIXED, mixed_send.at[peer[0]], mixed_all.at[g], peer).start()


    total_of(VALUES).wait_recv()
    value_head = jnp.concatenate(
        [unpack_block(value_all[i].astype(F32), head_size) for i in range(n_grp)], axis=0
    ).astype(BF16)
    loads["out"].wait()
    total_of(MIXED).wait_recv()
    mixed_head = mixed_all[...].reshape(n_grp * rows, width)
    pooled = dot(mixed_head, value_head).astype(BF16)
    partial_embed = dot(pooled, w_out[...])
    embed_send[...] = partial_embed.reshape(n_grp, rows, width).astype(BF16)
    embed_all[pl.ds(g, 1)] = embed_send[pl.ds(g, 1)]
    for step in GRP_STEPS:
        peer = grp_peer(step)
        copy(EMBED, embed_send.at[peer[0]], embed_all.at[g], peer).start()

    total_of(EMBED).wait_recv()
    unit_image, inverse_image = unit_rows(jnp.sum(embed_all[...].astype(F32), axis=0))
    unit_image_b = unit_image.astype(BF16)
    image_send[...] = unit_image_b
    image_all[pl.ds(b, 1)] = unit_image_b[None]
    odd = lax.rem(lax.div(g, 2), 2)
    for even_target, odd_target in zip(BLK_ORDER, BLK_ORDER_ODD, strict=True):
        target = jnp.where(odd == 0, even_target, odd_target)

        @pl.when(b != target)
        def send_image(target=target):
            copy(IMAGE, image_send, image_all.at[b], (g, target)).start()

    total_of(TEXT_PAIRS).wait_recv()
    all_texts = text_all[...].reshape(n_blk * rows, width)

    slopes = slopes_of(dot_rows(unit_image_b, all_texts), first_text)
    grads_ref[:rows] = chain_back(10.0 * dot(slopes, all_texts), unit_image, inverse_image)

    total_of(IMAGE).wait_recv()
    all_images = image_all[...].reshape(n_blk * rows, width)
    slopes = slopes_of(dot_rows(unit_text_b, all_images), b * rows)
    grads_ref[rows:] = chain_back(10.0 * dot(slopes, all_images), unit_text, inverse_text)

    for phase in range(PHASES):
        total_of(phase).wait_send()


def solution(mesh):
    n_grp, n_blk = mesh.shape["grp"], mesh.shape["blk"]

    def local(patches, probe, w_key, w_value, w_out, texts):
        rows, patch_count, width = patches.shape
        depth = w_key.shape[0]
        packed = 2 * depth // 3
        hbm = pl.BlockSpec(memory_space=pltpu.HBM)
        vmem = pl.BlockSpec(memory_space=pltpu.VMEM)
        operands = (patches.reshape(rows * patch_count, width), probe, w_key, w_value, w_out, texts)
        grads = pl.pallas_call(
            lambda *refs: kernel(n_grp, n_blk, *refs),
            out_shape=pltpu.VMEM((2 * rows, width), F32),
            in_specs=[hbm] * len(operands),
            out_specs=vmem,
            scratch_shapes=[
                pltpu.VMEM((rows * patch_count, width), BF16),
                pltpu.VMEM((width,), BF16),
                pltpu.VMEM((depth, width), BF16),
                pltpu.VMEM((depth, width), BF16),
                pltpu.VMEM((depth, width), BF16),
                pltpu.VMEM((rows, width), BF16),
                pltpu.VMEM((HEADS, LANES), F32),
                pltpu.VMEM((n_grp, HEADS, LANES), F32),
                pltpu.VMEM((n_grp, packed, LANES), BF16),
                pltpu.VMEM((n_grp, packed, LANES), BF16),
                pltpu.VMEM((n_blk // 2, 2, rows, width), BF16),
                pltpu.VMEM((n_grp, rows, width), BF16),
                pltpu.VMEM((n_grp, rows, width), BF16),
                pltpu.VMEM((n_grp, rows, width), BF16),
                pltpu.VMEM((n_grp, rows, width), BF16),
                pltpu.VMEM((rows, width), BF16),
                pltpu.VMEM((n_blk, rows, width), BF16),
                pltpu.SemaphoreType.DMA((6,)),
                pltpu.SemaphoreType.DMA((PHASES,)),
                pltpu.SemaphoreType.DMA((PHASES,)),
            ],
            compiler_params=pltpu.CompilerParams(
                collective_id=0, has_side_effects=True, vmem_limit_bytes=24 << 20
            ),
        )(*(pltpu.with_memory_space_constraint(x, pltpu.HBM) for x in operands))
        return grads[:rows], grads[rows:]

    split = P(("grp", "blk"), None)
    in_specs = (P(("grp", "blk"), None, None), P(), P("grp", None), P("grp", None), P("grp", None), split)
    return jax.shard_map(local, mesh=mesh, in_specs=in_specs, out_specs=(split, split), check_vma=False)
```

```python
import math

import jax
import jax.numpy as jnp
from jax import lax
from jax.experimental import pallas as pl
from jax.experimental.pallas import tpu as pltpu
from jax.sharding import PartitionSpec as P

HEADS = 16
MESH = pl.DeviceIdType.MESH
LANES = 128
F32 = jnp.float32
BF16 = jnp.bfloat16
GRP_STEPS = (11, 15, 7, 10, 14, 6, 9, 13, 5, 8, 12, 4, 3, 2, 1)
Z_STEPS = (4, 3, 5, 2, 6, 1, 7)
BLK_ORDER = (0, 8, 1, 9, 2, 10, 3, 11, 4, 7, 5, 6, 12, 15, 13, 14)
BLK_ORDER_HIGH = (0, 1, 2, 8, 9, 10, 3, 11, 4, 7, 5, 6, 12, 15, 13, 14)
KEYS, VALUES, TEXT_ONE, TEXT_PAIRS, MIXED, EMBED, IMAGE = 0, 1, 2, 3, 4, 5, 6
PHASES = 7


def dot_rows(left, right):
    return lax.dot_general(left, right, (((1,), (1,)), ((), ())), preferred_element_type=F32)


def dot(left, right):
    return lax.dot_general(left, right, (((1,), (0,)), ((), ())), preferred_element_type=F32)


def unit_rows(values):
    inverse = lax.rsqrt(jnp.sum(values * values, axis=1, keepdims=True) + 1e-06)
    return values * inverse, inverse


def chain_back(grad_unit, unit_f, inverse):
    inner = jnp.sum(unit_f * grad_unit, axis=1, keepdims=True)
    return (grad_unit - unit_f * inner) * inverse


def slopes_of(logits, first_row):
    rows, columns = logits.shape
    row = lax.broadcasted_iota(jnp.int32, (rows, columns), 0) + first_row
    column = lax.broadcasted_iota(jnp.int32, (rows, columns), 1)
    target = jnp.where(row == column, 1.0, 0.0)
    return (jax.nn.sigmoid(10.0 * logits - 2.0) - target).astype(BF16)


def pack_block(block):
    size = block.shape[1]
    low, room = 2 * size // 3, LANES - size
    rest = block[low:]
    blank = jnp.zeros((size - low, 2 * room - size), F32)
    over = jnp.concatenate([rest[:, room:], blank], axis=1)
    right = jnp.concatenate([rest[:, :room], over], axis=0)
    return jnp.concatenate([block[:low], right], axis=1)


def unpack_block(packed, size):
    half, room = size // 3, LANES - size
    rest = jnp.concatenate([packed[:half, size:], packed[half:, size : 2 * size - room]], axis=1)
    return jnp.concatenate([packed[:, :size], rest], axis=0)


def kernel(
    n_grp,
    n_blk,
    patches_hbm,
    probe_hbm,
    w_key_hbm,
    w_value_hbm,
    w_out_hbm,
    texts_hbm,
    grads_ref,
    patches,
    probe_local,
    w_key,
    w_value,
    w_out,
    texts,
    key_send,
    key_all,
    value_send,
    value_all,
    text_all,
    mixed_send,
    mixed_all,
    embed_send,
    embed_all,
    image_send,
    image_all,
    load_sem,
    send_sem,
    recv_sem,
):
    g, b = lax.axis_index("grp"), lax.axis_index("blk")
    rows = texts.shape[0]
    width = texts.shape[1]
    head_size = width // HEADS
    patch_count = patches.shape[0] // rows
    n_z = n_blk // 2
    z, x_hi = lax.rem(b, n_z), lax.div(b, n_z)
    first_text = (z * 2 + x_hi) * rows

    def grp_peer(step):
        return (jnp.bitwise_xor(g, step), b)

    def blk_peer(turn, step):
        return (g, lax.rem(x_hi + turn, 2) * n_z + lax.rem(z + step, n_z))

    barrier = pltpu.get_barrier_semaphore()
    for step in GRP_STEPS:
        pl.semaphore_signal(barrier, inc=1, device_id=grp_peer(step), device_id_type=MESH)
    blk_peers = [blk_peer(1, step) for step in Z_STEPS + (0,)] + [blk_peer(0, step) for step in Z_STEPS]
    for peer in blk_peers:
        pl.semaphore_signal(barrier, inc=1, device_id=peer, device_id_type=MESH)

    loads = {}
    for index, (name, source, target) in enumerate(
        (
            ("probe", probe_hbm, probe_local),
            ("key", w_key_hbm, w_key),
            ("text", texts_hbm, texts),
            ("value", w_value_hbm, w_value),
            ("patches", patches_hbm, patches),
            ("out", w_out_hbm, w_out),
        )
    ):
        loads[name] = pltpu.make_async_copy(source, target, load_sem.at[index])
        loads[name].start()

    def copy(phase, source, target, device):
        return pltpu.make_async_remote_copy(
            src_ref=source,
            dst_ref=target,
            send_sem=send_sem.at[phase],
            recv_sem=recv_sem.at[phase],
            device_id=device,
            device_id_type=MESH,
        )

    def total_of(phase):
        many = {
            KEYS: key_all.at[pl.ds(0, n_grp - 1)],
            VALUES: value_all.at[pl.ds(0, n_grp - 1)],
            TEXT_ONE: text_all.at[0, 0],
            TEXT_PAIRS: text_all.at[pl.ds(0, n_z - 1)],
            MIXED: mixed_all.at[pl.ds(0, n_grp - 1)],
            EMBED: embed_all.at[pl.ds(0, n_grp - 1)],
            IMAGE: image_all.at[pl.ds(0, n_blk - 1)],
        }[phase]
        return copy(phase, many, many, (g, b))

    column = lax.broadcasted_iota(jnp.int32, (HEADS, width), 1)
    head = lax.broadcasted_iota(jnp.int32, (HEADS, width), 0)
    owned = (column >= head * head_size) & (column < (head + 1) * head_size)
    loads["probe"].wait()
    probe = jnp.broadcast_to(probe_local[...].astype(F32)[None, :], (HEADS, width))
    query_table = jnp.where(owned, probe, 0.0).astype(BF16)
    loads["key"].wait()
    keys = dot_rows(query_table, w_key[...])
    key_send[...] = jnp.zeros(key_send.shape, F32)
    key_send[:, :head_size] = keys
    key_all[pl.ds(g, 1)] = key_send[...][None]

    loads["text"].wait()
    unit_text, inverse_text = unit_rows(texts[...].astype(F32))
    unit_text_b = unit_text.astype(BF16)
    text_all[pl.ds(z, 1), pl.ds(x_hi, 1)] = unit_text_b[None, None]

    pl.semaphore_wait(barrier, n_grp + n_blk - 2)
    for step in GRP_STEPS:
        copy(KEYS, key_send, key_all.at[g], grp_peer(step)).start()
    copy(TEXT_ONE, text_all.at[z, x_hi], text_all.at[z, x_hi], blk_peer(1, 0)).start()

    loads["value"].wait()
    value_f = w_value[...].astype(F32)
    for h in range(HEADS):
        value_send[h] = pack_block(value_f[:, h * head_size : (h + 1) * head_size]).astype(BF16)
    value_all[pl.ds(g, 1)] = value_send[pl.ds(g, 1)]
    for step in GRP_STEPS[::-1]:
        peer = grp_peer(step)
        copy(VALUES, value_send.at[peer[0]], value_all.at[g], peer).start()

    loads["patches"].wait()
    total_of(KEYS).wait_recv()
    total_of(TEXT_ONE).wait_recv()
    for step in Z_STEPS:
        copy(TEXT_PAIRS, text_all.at[z], text_all.at[z], blk_peer(0, step)).start()
    probe_keys = jnp.concatenate([key_all[i][:, :head_size] for i in range(n_grp)], axis=1)
    top_part = probe_keys.astype(BF16)
    rest = probe_keys - top_part.astype(F32)
    mid_part = rest.astype(BF16)
    low_part = (rest - mid_part.astype(F32)).astype(BF16)
    stacked = jnp.concatenate([top_part, mid_part, low_part], axis=0)
    parts = dot_rows(stacked, patches[...])
    scores = (parts[:HEADS] + parts[HEADS : 2 * HEADS] + parts[2 * HEADS :]) * (
        1.0 / math.sqrt(head_size)
    )
    flat = rows * patch_count
    spread = jnp.broadcast_to(scores[:, None, :], (HEADS, rows, flat)).reshape(HEADS * rows, flat)
    image = lax.broadcasted_iota(jnp.int32, (HEADS, rows, flat), 1).reshape(HEADS * rows, flat)
    position = lax.broadcasted_iota(jnp.int32, (HEADS * rows, flat), 1)
    inside = (position >= image * patch_count) & (position < (image + 1) * patch_count)
    spread = jnp.where(inside, spread, -jnp.inf)
    expo = jnp.exp(spread - jnp.max(spread, axis=1, keepdims=True)).astype(BF16)
    denominator = jnp.sum(expo.astype(F32), axis=1, keepdims=True)
    mixed = dot(expo, patches[...]) * (1.0 / denominator)
    mixed_send[...] = mixed.reshape(HEADS, rows, width).astype(BF16)
    mixed_all[pl.ds(g, 1)] = mixed_send[pl.ds(g, 1)]
    for step in GRP_STEPS:
        peer = grp_peer(step)
        copy(MIXED, mixed_send.at[peer[0]], mixed_all.at[g], peer).start()


    total_of(VALUES).wait_recv()
    value_head = jnp.concatenate(
        [unpack_block(value_all[i].astype(F32), head_size) for i in range(n_grp)], axis=0
    ).astype(BF16)
    loads["out"].wait()
    total_of(MIXED).wait_recv()
    mixed_head = mixed_all[...].reshape(n_grp * rows, width)
    pooled = dot(mixed_head, value_head).astype(BF16)
    partial_embed = dot(pooled, w_out[...])
    embed_send[...] = partial_embed.reshape(n_grp, rows, width).astype(BF16)
    embed_all[pl.ds(g, 1)] = embed_send[pl.ds(g, 1)]
    for step in GRP_STEPS:
        peer = grp_peer(step)
        copy(EMBED, embed_send.at[peer[0]], embed_all.at[g], peer).start()

    total_of(EMBED).wait_recv()
    unit_image, inverse_image = unit_rows(jnp.sum(embed_all[...].astype(F32), axis=0))
    unit_image_b = unit_image.astype(BF16)
    image_send[...] = unit_image_b
    image_all[pl.ds(b, 1)] = unit_image_b[None]
    for low_target, high_target in zip(BLK_ORDER, BLK_ORDER_HIGH, strict=True):
        target = jnp.where(x_hi == 0, low_target, high_target)

        @pl.when(b != target)
        def send_image(target=target):
            copy(IMAGE, image_send, image_all.at[b], (g, target)).start()

    total_of(TEXT_PAIRS).wait_recv()
    all_texts = text_all[...].reshape(n_blk * rows, width)

    slopes = slopes_of(dot_rows(unit_image_b, all_texts), first_text)
    grads_ref[:rows] = chain_back(10.0 * dot(slopes, all_texts), unit_image, inverse_image)

    total_of(IMAGE).wait_recv()
    all_images = image_all[...].reshape(n_blk * rows, width)
    slopes = slopes_of(dot_rows(unit_text_b, all_images), b * rows)
    grads_ref[rows:] = chain_back(10.0 * dot(slopes, all_images), unit_text, inverse_text)

    for phase in range(PHASES):
        total_of(phase).wait_send()


def solution(mesh):
    n_grp, n_blk = mesh.shape["grp"], mesh.shape["blk"]

    def local(patches, probe, w_key, w_value, w_out, texts):
        rows, patch_count, width = patches.shape
        depth = w_key.shape[0]
        packed = 2 * depth // 3
        hbm = pl.BlockSpec(memory_space=pltpu.HBM)
        vmem = pl.BlockSpec(memory_space=pltpu.VMEM)
        operands = (patches.reshape(rows * patch_count, width), probe, w_key, w_value, w_out, texts)
        grads = pl.pallas_call(
            lambda *refs: kernel(n_grp, n_blk, *refs),
            out_shape=pltpu.VMEM((2 * rows, width), F32),
            in_specs=[hbm] * len(operands),
            out_specs=vmem,
            scratch_shapes=[
                pltpu.VMEM((rows * patch_count, width), BF16),
                pltpu.VMEM((width,), BF16),
                pltpu.VMEM((depth, width), BF16),
                pltpu.VMEM((depth, width), BF16),
                pltpu.VMEM((depth, width), BF16),
                pltpu.VMEM((rows, width), BF16),
                pltpu.VMEM((HEADS, LANES), F32),
                pltpu.VMEM((n_grp, HEADS, LANES), F32),
                pltpu.VMEM((n_grp, packed, LANES), BF16),
                pltpu.VMEM((n_grp, packed, LANES), BF16),
                pltpu.VMEM((n_blk // 2, 2, rows, width), BF16),
                pltpu.VMEM((n_grp, rows, width), BF16),
                pltpu.VMEM((n_grp, rows, width), BF16),
                pltpu.VMEM((n_grp, rows, width), BF16),
                pltpu.VMEM((n_grp, rows, width), BF16),
                pltpu.VMEM((rows, width), BF16),
                pltpu.VMEM((n_blk, rows, width), BF16),
                pltpu.SemaphoreType.DMA((6,)),
                pltpu.SemaphoreType.DMA((PHASES,)),
                pltpu.SemaphoreType.DMA((PHASES,)),
            ],
            compiler_params=pltpu.CompilerParams(
                collective_id=0, has_side_effects=True, vmem_limit_bytes=24 << 20
            ),
        )(*(pltpu.with_memory_space_constraint(x, pltpu.HBM) for x in operands))
        return grads[:rows], grads[rows:]

    split = P(("grp", "blk"), None)
    in_specs = (P(("grp", "blk"), None, None), P(), P("grp", None), P("grp", None), P("grp", None), split)
    return jax.shard_map(local, mesh=mesh, in_specs=in_specs, out_specs=(split, split), check_vma=False)
```

```python
import math

import jax
import jax.numpy as jnp
from jax import lax
from jax.experimental import pallas as pl
from jax.experimental.pallas import tpu as pltpu
from jax.sharding import PartitionSpec as P

HEADS = 16
MESH = pl.DeviceIdType.MESH
LANES = 128
F32 = jnp.float32
BF16 = jnp.bfloat16
GRP_STEPS = (11, 15, 7, 10, 14, 6, 9, 13, 5, 8, 12, 4, 3, 2, 1)
Z_STEPS = (4, 3, 5, 2, 6, 1, 7)
BLK_ORDER = (0, 8, 1, 9, 2, 10, 3, 11, 4, 7, 5, 6, 12, 15, 13, 14)
BLK_ORDER_HIGH = (0, 1, 2, 8, 9, 10, 3, 11, 4, 7, 5, 6, 12, 15, 13, 14)
KEYS, VALUES, TEXT_ONE, TEXT_PAIRS, MIXED, EMBED, IMAGE = 0, 1, 2, 3, 4, 5, 6
PHASES = 7


def dot_rows(left, right):
    return lax.dot_general(left, right, (((1,), (1,)), ((), ())), preferred_element_type=F32)


def dot(left, right):
    return lax.dot_general(left, right, (((1,), (0,)), ((), ())), preferred_element_type=F32)


def unit_rows(values):
    inverse = lax.rsqrt(jnp.sum(values * values, axis=1, keepdims=True) + 1e-06)
    return values * inverse, inverse


def chain_back(grad_unit, unit_f, inverse):
    inner = jnp.sum(unit_f * grad_unit, axis=1, keepdims=True)
    return (grad_unit - unit_f * inner) * inverse


def slopes_of(logits, first_row):
    rows, columns = logits.shape
    row = lax.broadcasted_iota(jnp.int32, (rows, columns), 0) + first_row
    column = lax.broadcasted_iota(jnp.int32, (rows, columns), 1)
    target = jnp.where(row == column, 1.0, 0.0)
    return (jax.nn.sigmoid(10.0 * logits - 2.0) - target).astype(BF16)


def pack_block(block):
    size = block.shape[1]
    low, room = 2 * size // 3, LANES - size
    rest = block[low:]
    blank = jnp.zeros((size - low, 2 * room - size), F32)
    over = jnp.concatenate([rest[:, room:], blank], axis=1)
    right = jnp.concatenate([rest[:, :room], over], axis=0)
    return jnp.concatenate([block[:low], right], axis=1)


def unpack_block(packed, size):
    half, room = size // 3, LANES - size
    rest = jnp.concatenate([packed[:half, size:], packed[half:, size : 2 * size - room]], axis=1)
    return jnp.concatenate([packed[:, :size], rest], axis=0)


def kernel(
    n_grp,
    n_blk,
    patches_hbm,
    probe_hbm,
    w_key_hbm,
    w_value_hbm,
    w_out_hbm,
    texts_hbm,
    grads_ref,
    patches,
    probe_local,
    w_key,
    w_value,
    w_out,
    texts,
    key_send,
    key_all,
    value_send,
    value_all,
    text_all,
    mixed_send,
    mixed_all,
    embed_send,
    embed_all,
    image_send,
    image_all,
    load_sem,
    send_sem,
    recv_sem,
):
    g, b = lax.axis_index("grp"), lax.axis_index("blk")
    rows = texts.shape[0]
    width = texts.shape[1]
    head_size = width // HEADS
    patch_count = patches.shape[0] // rows
    n_z = n_blk // 2
    z, x_hi = lax.rem(b, n_z), lax.div(b, n_z)
    first_text = (z * 2 + x_hi) * rows

    def grp_peer(step):
        return (jnp.bitwise_xor(g, step), b)

    def blk_peer(turn, step):
        return (g, lax.rem(x_hi + turn, 2) * n_z + lax.rem(z + step, n_z))

    barrier = pltpu.get_barrier_semaphore()
    for step in GRP_STEPS:
        pl.semaphore_signal(barrier, inc=1, device_id=grp_peer(step), device_id_type=MESH)
    blk_peers = [blk_peer(1, step) for step in Z_STEPS + (0,)] + [blk_peer(0, step) for step in Z_STEPS]
    for peer in blk_peers:
        pl.semaphore_signal(barrier, inc=1, device_id=peer, device_id_type=MESH)

    loads = {}
    for index, (name, source, target) in enumerate(
        (
            ("probe", probe_hbm, probe_local),
            ("key", w_key_hbm, w_key),
            ("text", texts_hbm, texts),
            ("value", w_value_hbm, w_value),
            ("patches", patches_hbm, patches),
            ("out", w_out_hbm, w_out),
        )
    ):
        loads[name] = pltpu.make_async_copy(source, target, load_sem.at[index])
        loads[name].start()

    def copy(phase, source, target, device):
        return pltpu.make_async_remote_copy(
            src_ref=source,
            dst_ref=target,
            send_sem=send_sem.at[phase],
            recv_sem=recv_sem.at[phase],
            device_id=device,
            device_id_type=MESH,
        )

    def total_of(phase):
        many = {
            KEYS: key_all.at[pl.ds(0, n_grp - 1)],
            VALUES: value_all.at[pl.ds(0, n_grp - 1)],
            TEXT_ONE: text_all.at[0, 0],
            TEXT_PAIRS: text_all.at[pl.ds(0, n_z - 1)],
            MIXED: mixed_all.at[pl.ds(0, n_grp - 1)],
            EMBED: embed_all.at[pl.ds(0, n_grp - 1)],
            IMAGE: image_all.at[pl.ds(0, n_blk - 1)],
        }[phase]
        return copy(phase, many, many, (g, b))

    column = lax.broadcasted_iota(jnp.int32, (HEADS, width), 1)
    head = lax.broadcasted_iota(jnp.int32, (HEADS, width), 0)
    owned = (column >= head * head_size) & (column < (head + 1) * head_size)
    loads["probe"].wait()
    probe = jnp.broadcast_to(probe_local[...].astype(F32)[None, :], (HEADS, width))
    query_table = jnp.where(owned, probe, 0.0).astype(BF16)
    loads["key"].wait()
    keys = dot_rows(query_table, w_key[...])
    key_send[...] = jnp.zeros(key_send.shape, F32)
    key_send[:, :head_size] = keys
    key_all[pl.ds(g, 1)] = key_send[...][None]

    loads["text"].wait()
    unit_text, inverse_text = unit_rows(texts[...].astype(F32))
    unit_text_b = unit_text.astype(BF16)
    text_all[pl.ds(z, 1), pl.ds(x_hi, 1)] = unit_text_b[None, None]

    pl.semaphore_wait(barrier, n_grp + n_blk - 2)
    for step in GRP_STEPS:
        copy(KEYS, key_send, key_all.at[g], grp_peer(step)).start()
    copy(TEXT_ONE, text_all.at[z, x_hi], text_all.at[z, x_hi], blk_peer(1, 0)).start()

    loads["value"].wait()
    value_f = w_value[...].astype(F32)
    for h in range(HEADS):
        value_send[h] = pack_block(value_f[:, h * head_size : (h + 1) * head_size]).astype(BF16)
    value_all[pl.ds(g, 1)] = value_send[pl.ds(g, 1)]
    for step in GRP_STEPS[::-1]:
        peer = grp_peer(step)
        copy(VALUES, value_send.at[peer[0]], value_all.at[g], peer).start()

    loads["patches"].wait()
    total_of(KEYS).wait_recv()
    probe_keys = jnp.concatenate([key_all[i][:, :head_size] for i in range(n_grp)], axis=1)
    top_part = probe_keys.astype(BF16)
    rest = probe_keys - top_part.astype(F32)
    mid_part = rest.astype(BF16)
    low_part = (rest - mid_part.astype(F32)).astype(BF16)
    stacked = jnp.concatenate([top_part, mid_part, low_part], axis=0)
    parts = dot_rows(stacked, patches[...])
    scores = (parts[:HEADS] + parts[HEADS : 2 * HEADS] + parts[2 * HEADS :]) * (
        1.0 / math.sqrt(head_size)
    )
    flat = rows * patch_count
    spread = jnp.broadcast_to(scores[:, None, :], (HEADS, rows, flat)).reshape(HEADS * rows, flat)
    image = lax.broadcasted_iota(jnp.int32, (HEADS, rows, flat), 1).reshape(HEADS * rows, flat)
    position = lax.broadcasted_iota(jnp.int32, (HEADS * rows, flat), 1)
    inside = (position >= image * patch_count) & (position < (image + 1) * patch_count)
    spread = jnp.where(inside, spread, -jnp.inf)
    expo = jnp.exp(spread - jnp.max(spread, axis=1, keepdims=True)).astype(BF16)
    denominator = jnp.sum(expo.astype(F32), axis=1, keepdims=True)
    mixed = dot(expo, patches[...]) * (1.0 / denominator)
    mixed_send[...] = mixed.reshape(HEADS, rows, width).astype(BF16)
    mixed_all[pl.ds(g, 1)] = mixed_send[pl.ds(g, 1)]
    for step in GRP_STEPS:
        peer = grp_peer(step)
        copy(MIXED, mixed_send.at[peer[0]], mixed_all.at[g], peer).start()


    total_of(VALUES).wait_recv()
    total_of(TEXT_ONE).wait_recv()
    for step in Z_STEPS:
        copy(TEXT_PAIRS, text_all.at[z], text_all.at[z], blk_peer(0, step)).start()
    value_head = jnp.concatenate(
        [unpack_block(value_all[i].astype(F32), head_size) for i in range(n_grp)], axis=0
    ).astype(BF16)
    loads["out"].wait()
    total_of(MIXED).wait_recv()
    mixed_head = mixed_all[...].reshape(n_grp * rows, width)
    pooled = dot(mixed_head, value_head).astype(BF16)
    partial_embed = dot(pooled, w_out[...])
    embed_send[...] = partial_embed.reshape(n_grp, rows, width).astype(BF16)
    embed_all[pl.ds(g, 1)] = embed_send[pl.ds(g, 1)]
    for step in GRP_STEPS:
        peer = grp_peer(step)
        copy(EMBED, embed_send.at[peer[0]], embed_all.at[g], peer).start()

    total_of(EMBED).wait_recv()
    unit_image, inverse_image = unit_rows(jnp.sum(embed_all[...].astype(F32), axis=0))
    unit_image_b = unit_image.astype(BF16)
    image_send[...] = unit_image_b
    image_all[pl.ds(b, 1)] = unit_image_b[None]
    for low_target, high_target in zip(BLK_ORDER, BLK_ORDER_HIGH, strict=True):
        target = jnp.where(x_hi == 0, low_target, high_target)

        @pl.when(b != target)
        def send_image(target=target):
            copy(IMAGE, image_send, image_all.at[b], (g, target)).start()

    total_of(TEXT_PAIRS).wait_recv()
    all_texts = text_all[...].reshape(n_blk * rows, width)

    slopes = slopes_of(dot_rows(unit_image_b, all_texts), first_text)
    grads_ref[:rows] = chain_back(10.0 * dot(slopes, all_texts), unit_image, inverse_image)

    total_of(IMAGE).wait_recv()
    all_images = image_all[...].reshape(n_blk * rows, width)
    slopes = slopes_of(dot_rows(unit_text_b, all_images), b * rows)
    grads_ref[rows:] = chain_back(10.0 * dot(slopes, all_images), unit_text, inverse_text)

    for phase in range(PHASES):
        total_of(phase).wait_send()


def solution(mesh):
    n_grp, n_blk = mesh.shape["grp"], mesh.shape["blk"]

    def local(patches, probe, w_key, w_value, w_out, texts):
        rows, patch_count, width = patches.shape
        depth = w_key.shape[0]
        packed = 2 * depth // 3
        hbm = pl.BlockSpec(memory_space=pltpu.HBM)
        vmem = pl.BlockSpec(memory_space=pltpu.VMEM)
        operands = (patches.reshape(rows * patch_count, width), probe, w_key, w_value, w_out, texts)
        grads = pl.pallas_call(
            lambda *refs: kernel(n_grp, n_blk, *refs),
            out_shape=pltpu.VMEM((2 * rows, width), F32),
            in_specs=[hbm] * len(operands),
            out_specs=vmem,
            scratch_shapes=[
                pltpu.VMEM((rows * patch_count, width), BF16),
                pltpu.VMEM((width,), BF16),
                pltpu.VMEM((depth, width), BF16),
                pltpu.VMEM((depth, width), BF16),
                pltpu.VMEM((depth, width), BF16),
                pltpu.VMEM((rows, width), BF16),
                pltpu.VMEM((HEADS, LANES), F32),
                pltpu.VMEM((n_grp, HEADS, LANES), F32),
                pltpu.VMEM((n_grp, packed, LANES), BF16),
                pltpu.VMEM((n_grp, packed, LANES), BF16),
                pltpu.VMEM((n_blk // 2, 2, rows, width), BF16),
                pltpu.VMEM((n_grp, rows, width), BF16),
                pltpu.VMEM((n_grp, rows, width), BF16),
                pltpu.VMEM((n_grp, rows, width), BF16),
                pltpu.VMEM((n_grp, rows, width), BF16),
                pltpu.VMEM((rows, width), BF16),
                pltpu.VMEM((n_blk, rows, width), BF16),
                pltpu.SemaphoreType.DMA((6,)),
                pltpu.SemaphoreType.DMA((PHASES,)),
                pltpu.SemaphoreType.DMA((PHASES,)),
            ],
            compiler_params=pltpu.CompilerParams(
                collective_id=0, has_side_effects=True, vmem_limit_bytes=24 << 20
            ),
        )(*(pltpu.with_memory_space_constraint(x, pltpu.HBM) for x in operands))
        return grads[:rows], grads[rows:]

    split = P(("grp", "blk"), None)
    in_specs = (P(("grp", "blk"), None, None), P(), P("grp", None), P("grp", None), P("grp", None), split)
    return jax.shard_map(local, mesh=mesh, in_specs=in_specs, out_specs=(split, split), check_vma=False)
```

```python
import math

import jax
import jax.numpy as jnp
from jax import lax
from jax.experimental import pallas as pl
from jax.experimental.pallas import tpu as pltpu
from jax.sharding import PartitionSpec as P

HEADS = 16
MESH = pl.DeviceIdType.MESH
LANES = 128
F32 = jnp.float32
BF16 = jnp.bfloat16
GRP_STEPS = (11, 15, 7, 10, 14, 6, 9, 13, 5, 8, 12, 4, 3, 2, 1)
Z_STEPS = (4, 3, 5, 2, 6, 1, 7)
BLK_ORDER = (0, 8, 1, 9, 2, 10, 3, 11, 4, 7, 5, 6, 12, 15, 13, 14)
BLK_ORDER_HIGH = (0, 1, 2, 8, 9, 10, 3, 11, 4, 7, 5, 6, 12, 15, 13, 14)
KEYS, VALUES, TEXT_ONE, TEXT_PAIRS, MIXED, EMBED, IMAGE = 0, 1, 2, 3, 4, 5, 6
PHASES = 7


def dot_rows(left, right):
    return lax.dot_general(left, right, (((1,), (1,)), ((), ())), preferred_element_type=F32)


def dot(left, right):
    return lax.dot_general(left, right, (((1,), (0,)), ((), ())), preferred_element_type=F32)


def unit_rows(values):
    inverse = lax.rsqrt(jnp.sum(values * values, axis=1, keepdims=True) + 1e-06)
    return values * inverse, inverse


def chain_back(grad_unit, unit_f, inverse):
    inner = jnp.sum(unit_f * grad_unit, axis=1, keepdims=True)
    return (grad_unit - unit_f * inner) * inverse


def slopes_of(logits, first_row):
    rows, columns = logits.shape
    row = lax.broadcasted_iota(jnp.int32, (rows, columns), 0) + first_row
    column = lax.broadcasted_iota(jnp.int32, (rows, columns), 1)
    target = jnp.where(row == column, 1.0, 0.0)
    return (jax.nn.sigmoid(10.0 * logits - 2.0) - target).astype(BF16)


def pack_block(block):
    size = block.shape[1]
    low, room = 2 * size // 3, LANES - size
    rest = block[low:]
    blank = jnp.zeros((size - low, 2 * room - size), F32)
    over = jnp.concatenate([rest[:, room:], blank], axis=1)
    right = jnp.concatenate([rest[:, :room], over], axis=0)
    return jnp.concatenate([block[:low], right], axis=1)


def unpack_block(packed, size):
    half, room = size // 3, LANES - size
    rest = jnp.concatenate([packed[:half, size:], packed[half:, size : 2 * size - room]], axis=1)
    return jnp.concatenate([packed[:, :size], rest], axis=0)


def kernel(
    n_grp,
    n_blk,
    patches_hbm,
    probe_hbm,
    w_key_hbm,
    w_value_hbm,
    w_out_hbm,
    texts_hbm,
    grads_ref,
    patches,
    probe_local,
    w_key,
    w_value,
    w_out,
    texts,
    key_send,
    key_all,
    value_send,
    value_all,
    text_all,
    mixed_send,
    mixed_all,
    embed_send,
    embed_all,
    image_send,
    image_all,
    load_sem,
    send_sem,
    recv_sem,
):
    g, b = lax.axis_index("grp"), lax.axis_index("blk")
    rows = texts.shape[0]
    width = texts.shape[1]
    head_size = width // HEADS
    patch_count = patches.shape[0] // rows
    n_z = n_blk // 2
    z, x_hi = lax.rem(b, n_z), lax.div(b, n_z)
    first_text = (z * 2 + x_hi) * rows

    def grp_peer(step):
        return (jnp.bitwise_xor(g, step), b)

    def blk_peer(turn, step):
        return (g, lax.rem(x_hi + turn, 2) * n_z + lax.rem(z + step, n_z))

    barrier = pltpu.get_barrier_semaphore()
    for step in GRP_STEPS:
        pl.semaphore_signal(barrier, inc=1, device_id=grp_peer(step), device_id_type=MESH)
    blk_peers = [blk_peer(1, step) for step in Z_STEPS + (0,)] + [blk_peer(0, step) for step in Z_STEPS]
    for peer in blk_peers:
        pl.semaphore_signal(barrier, inc=1, device_id=peer, device_id_type=MESH)

    loads = {}
    for index, (name, source, target) in enumerate(
        (
            ("probe", probe_hbm, probe_local),
            ("key", w_key_hbm, w_key),
            ("text", texts_hbm, texts),
            ("value", w_value_hbm, w_value),
            ("patches", patches_hbm, patches),
            ("out", w_out_hbm, w_out),
        )
    ):
        loads[name] = pltpu.make_async_copy(source, target, load_sem.at[index])
        loads[name].start()

    def copy(phase, source, target, device):
        return pltpu.make_async_remote_copy(
            src_ref=source,
            dst_ref=target,
            send_sem=send_sem.at[phase],
            recv_sem=recv_sem.at[phase],
            device_id=device,
            device_id_type=MESH,
        )

    def total_of(phase):
        many = {
            KEYS: key_all.at[pl.ds(0, n_grp - 1)],
            VALUES: value_all.at[pl.ds(0, n_grp - 1)],
            TEXT_ONE: text_all.at[0, 0],
            TEXT_PAIRS: text_all.at[pl.ds(0, n_z - 1)],
            MIXED: mixed_all.at[pl.ds(0, n_grp - 1)],
            EMBED: embed_all.at[pl.ds(0, n_grp - 1)],
            IMAGE: image_all.at[pl.ds(0, n_blk - 1)],
        }[phase]
        return copy(phase, many, many, (g, b))

    column = lax.broadcasted_iota(jnp.int32, (HEADS, width), 1)
    head = lax.broadcasted_iota(jnp.int32, (HEADS, width), 0)
    owned = (column >= head * head_size) & (column < (head + 1) * head_size)
    loads["probe"].wait()
    probe = jnp.broadcast_to(probe_local[...].astype(F32)[None, :], (HEADS, width))
    query_table = jnp.where(owned, probe, 0.0).astype(BF16)
    loads["key"].wait()
    keys = dot_rows(query_table, w_key[...])
    key_send[...] = jnp.zeros(key_send.shape, F32)
    key_send[:, :head_size] = keys
    key_all[pl.ds(g, 1)] = key_send[...][None]

    loads["text"].wait()
    unit_text, inverse_text = unit_rows(texts[...].astype(F32))
    unit_text_b = unit_text.astype(BF16)
    text_all[pl.ds(z, 1), pl.ds(x_hi, 1)] = unit_text_b[None, None]

    pl.semaphore_wait(barrier, n_grp + n_blk - 2)
    for step in GRP_STEPS:
        copy(KEYS, key_send, key_all.at[g], grp_peer(step)).start()
    copy(TEXT_ONE, text_all.at[z, x_hi], text_all.at[z, x_hi], blk_peer(1, 0)).start()

    loads["value"].wait()
    value_f = w_value[...].astype(F32)
    for h in range(HEADS):
        value_send[h] = pack_block(value_f[:, h * head_size : (h + 1) * head_size]).astype(BF16)
    value_all[pl.ds(g, 1)] = value_send[pl.ds(g, 1)]
    for step in GRP_STEPS[::-1]:
        peer = grp_peer(step)
        copy(VALUES, value_send.at[peer[0]], value_all.at[g], peer).start()

    loads["patches"].wait()
    total_of(KEYS).wait_recv()
    probe_keys = jnp.concatenate([key_all[i][:, :head_size] for i in range(n_grp)], axis=1)
    top_part = probe_keys.astype(BF16)
    rest = probe_keys - top_part.astype(F32)
    mid_part = rest.astype(BF16)
    low_part = (rest - mid_part.astype(F32)).astype(BF16)
    stacked = jnp.concatenate([top_part, mid_part, low_part], axis=0)
    parts = dot_rows(stacked, patches[...])
    scores = (parts[:HEADS] + parts[HEADS : 2 * HEADS] + parts[2 * HEADS :]) * (
        1.0 / math.sqrt(head_size)
    )
    flat = rows * patch_count
    spread = jnp.broadcast_to(scores[:, None, :], (HEADS, rows, flat)).reshape(HEADS * rows, flat)
    image = lax.broadcasted_iota(jnp.int32, (HEADS, rows, flat), 1).reshape(HEADS * rows, flat)
    position = lax.broadcasted_iota(jnp.int32, (HEADS * rows, flat), 1)
    inside = (position >= image * patch_count) & (position < (image + 1) * patch_count)
    spread = jnp.where(inside, spread, -jnp.inf)
    expo = jnp.exp(spread - jnp.max(spread, axis=1, keepdims=True)).astype(BF16)
    denominator = jnp.sum(expo.astype(F32), axis=1, keepdims=True)
    mixed = dot(expo, patches[...]) * (1.0 / denominator)
    mixed_send[...] = mixed.reshape(HEADS, rows, width).astype(BF16)
    mixed_all[pl.ds(g, 1)] = mixed_send[pl.ds(g, 1)]
    for step in GRP_STEPS:
        peer = grp_peer(step)
        copy(MIXED, mixed_send.at[peer[0]], mixed_all.at[g], peer).start()


    total_of(VALUES).wait_recv()
    total_of(TEXT_ONE).wait_recv()
    for step in Z_STEPS:
        copy(TEXT_PAIRS, text_all.at[z], text_all.at[z], blk_peer(0, step)).start()
    value_head = jnp.concatenate(
        [unpack_block(value_all[i].astype(F32), head_size) for i in range(n_grp)], axis=0
    ).astype(BF16)
    loads["out"].wait()
    total_of(MIXED).wait_recv()
    mixed_head = mixed_all[...].reshape(n_grp * rows, width)
    pooled = dot(mixed_head, value_head).astype(BF16)
    partial_embed = dot(pooled, w_out[...])
    embed_send[...] = partial_embed.reshape(n_grp, rows, width).astype(BF16)
    embed_all[pl.ds(g, 1)] = embed_send[pl.ds(g, 1)]
    for step in GRP_STEPS:
        peer = grp_peer(step)
        copy(EMBED, embed_send.at[peer[0]], embed_all.at[g], peer).start()

    total_of(EMBED).wait_recv()
    embed = jnp.sum(embed_all[...].astype(F32), axis=0)
    image_send[...] = embed.astype(BF16)
    image_all[pl.ds(b, 1)] = image_send[...][None]
    for low_target, high_target in zip(BLK_ORDER, BLK_ORDER_HIGH, strict=True):
        target = jnp.where(x_hi == 0, low_target, high_target)

        @pl.when(b != target)
        def send_image(target=target):
            copy(IMAGE, image_send, image_all.at[b], (g, target)).start()

    unit_image, inverse_image = unit_rows(embed)
    unit_image_b = unit_image.astype(BF16)
    total_of(TEXT_PAIRS).wait_recv()
    all_texts = text_all[...].reshape(n_blk * rows, width)

    slopes = slopes_of(dot_rows(unit_image_b, all_texts), first_text)
    grads_ref[:rows] = chain_back(10.0 * dot(slopes, all_texts), unit_image, inverse_image)

    total_of(IMAGE).wait_recv()
    all_images = image_all[...].astype(F32).reshape(n_blk * rows, width)
    all_images = unit_rows(all_images)[0].astype(BF16)
    slopes = slopes_of(dot_rows(unit_text_b, all_images), b * rows)
    grads_ref[rows:] = chain_back(10.0 * dot(slopes, all_images), unit_text, inverse_text)

    for phase in range(PHASES):
        total_of(phase).wait_send()


def solution(mesh):
    n_grp, n_blk = mesh.shape["grp"], mesh.shape["blk"]

    def local(patches, probe, w_key, w_value, w_out, texts):
        rows, patch_count, width = patches.shape
        depth = w_key.shape[0]
        packed = 2 * depth // 3
        hbm = pl.BlockSpec(memory_space=pltpu.HBM)
        vmem = pl.BlockSpec(memory_space=pltpu.VMEM)
        operands = (patches.reshape(rows * patch_count, width), probe, w_key, w_value, w_out, texts)
        grads = pl.pallas_call(
            lambda *refs: kernel(n_grp, n_blk, *refs),
            out_shape=pltpu.VMEM((2 * rows, width), F32),
            in_specs=[hbm] * len(operands),
            out_specs=vmem,
            scratch_shapes=[
                pltpu.VMEM((rows * patch_count, width), BF16),
                pltpu.VMEM((width,), BF16),
                pltpu.VMEM((depth, width), BF16),
                pltpu.VMEM((depth, width), BF16),
                pltpu.VMEM((depth, width), BF16),
                pltpu.VMEM((rows, width), BF16),
                pltpu.VMEM((HEADS, LANES), F32),
                pltpu.VMEM((n_grp, HEADS, LANES), F32),
                pltpu.VMEM((n_grp, packed, LANES), BF16),
                pltpu.VMEM((n_grp, packed, LANES), BF16),
                pltpu.VMEM((n_blk // 2, 2, rows, width), BF16),
                pltpu.VMEM((n_grp, rows, width), BF16),
                pltpu.VMEM((n_grp, rows, width), BF16),
                pltpu.VMEM((n_grp, rows, width), BF16),
                pltpu.VMEM((n_grp, rows, width), BF16),
                pltpu.VMEM((rows, width), BF16),
                pltpu.VMEM((n_blk, rows, width), BF16),
                pltpu.SemaphoreType.DMA((6,)),
                pltpu.SemaphoreType.DMA((PHASES,)),
                pltpu.SemaphoreType.DMA((PHASES,)),
            ],
            compiler_params=pltpu.CompilerParams(
                collective_id=0, has_side_effects=True, vmem_limit_bytes=24 << 20
            ),
        )(*(pltpu.with_memory_space_constraint(x, pltpu.HBM) for x in operands))
        return grads[:rows], grads[rows:]

    split = P(("grp", "blk"), None)
    in_specs = (P(("grp", "blk"), None, None), P(), P("grp", None), P("grp", None), P("grp", None), split)
    return jax.shard_map(local, mesh=mesh, in_specs=in_specs, out_specs=(split, split), check_vma=False)
```
